512 devices in a mesh: row: 16 (over y, core), col: 32 (over x, z).
Axes of the slice: x: 4, y: 8, z: 8, core: 2. Of those that a mesh axis runs over, the one named last changes fastest.
Arguments:
- a_trail: bfloat16 [16384, 16384], P('row', 'col'), may hold values from -6 to 6
- a_panel: bfloat16 [16384, 512], P('row', 'col'), may hold values from -60 to 60
- l_panel: bfloat16 [16384, 512], P('row', 'col'), may hold values from -0.25 to 0.25
- a_diag: bfloat16 [512, 512], P('row'), may hold values from -6 to 6
- linv_diag: bfloat16 [512, 512], P('row'), as said below
Outputs:
- c_trail: bfloat16 [16384, 16384], P('row', 'col')
- c_panel: bfloat16 [16384, 512], P('row', 'col')
- c_diag: bfloat16 [512, 512], P('row', 'col')
- r_band: float32 [256, 256], P('row', 'col')
- q_block: float32 [16384, 256], P('row', 'col')
The draws below stay inside these ranges and needn't reach their ends.
Inputs may be any that keep to these rules, and one draw needn't show every extreme that they name: linv_diag is lower triangular with diagonal entries between 0.5 and 2.
All inputs are finite; a program needn't handle non-finite values.
Results may differ from the reference program's by a relative error of at most 0.015.
Values may be sent and summed in bfloat16 or wider, within the bound.
No kernel may reach another device: no remote copies, remote signals or barrier semaphores. Data moves between devices by JAX's collectives and lax.ppermute only.
A program may use at most 64 MiB of HBM per device.

```python
import math
import jax
import jax.numpy as jnp
from jax import lax

M = 16384
NB = 512
BW = 256
N_ROW = 16


def draw_linv_diag(key, part):
    key = jax.random.fold_in(key, 7)
    key_below, key_diag = jax.random.split(key)
    rows = lax.broadcasted_iota(jnp.int32, (NB, NB), 0)
    cols = lax.broadcasted_iota(jnp.int32, (NB, NB), 1)
    below = jax.random.normal(key_below, (NB, NB), jnp.float32) * (0.5 / math.sqrt(NB))
    diag_values = jnp.exp(jax.random.uniform(key_diag, (NB, 1), jnp.float32, math.log(0.5), math.log(2.0)))
    result = jnp.where(rows > cols, below, 0.0) + jnp.where(rows == cols, diag_values, 0.0)
    return result.astype(jnp.bfloat16)


def draw_a_panel(key, part):
    key = jax.random.fold_in(key, 11)
    rows = lax.broadcasted_iota(jnp.int32, (M, NB), 0).astype(jnp.float32)
    scale = jnp.exp(rows * (math.log(10.0) / M))
    values = jnp.clip(jax.random.normal(key, (M, NB), jnp.float32), -6.0, 6.0)
    return (values * scale).astype(jnp.bfloat16)


def levels(stream_key, dims, cuts, least, top_value):
    loudness = 1.0
    for position, shards_of in cuts:
        draws = jax.random.uniform(jax.random.fold_in(jax.random.fold_in(stream_key, 6), position), (shards_of,), jnp.float32, least / len(cuts), top_value / len(cuts))
        loudness = loudness * jnp.repeat(jnp.exp(draws), dims[position] // shards_of).reshape((-1,) + (1,) * (len(dims) - 1 - position))
    return loudness


def scatter_about(key, dims, spread, most, cuts=(), held_as=jnp.bfloat16):
    level = levels(key, dims, cuts, -0.22, 0.18) if cuts else 1.0
    values = jax.random.normal(key, dims, jnp.float32) * spread * level
    return jnp.minimum(jnp.maximum(values, -most), most).astype(held_as)


def setup_inputs(seed: int = 0) -> dict:
    streams_of = jax.random.split(jax.random.key(seed), 6)
    a_trail = scatter_about(streams_of[0], (M, M), 1.0, 6.0, ((0, 16), (1, 32)))
    a_panel = draw_a_panel(jax.random.fold_in(streams_of[5], 71), 0)
    l_panel = scatter_about(streams_of[2], (M, NB), NB ** -0.5, 0.25, ((0, 16), (1, 32)))
    a_diag = scatter_about(streams_of[3], (NB, NB), 1.0, 6.0, ((0, 16),))
    linv_diag = draw_linv_diag(jax.random.fold_in(streams_of[5], 71), 0)
    return {"a_trail": a_trail, "a_panel": a_panel, "l_panel": l_panel, "a_diag": a_diag, "linv_diag": linv_diag}


def reference(a_trail, a_panel, l_panel, a_diag, linv_diag):
    inner = jnp.dot(linv_diag.astype(jnp.float32), a_diag.astype(jnp.float32), preferred_element_type=jnp.float32).astype(jnp.bfloat16)
    congruent = jnp.dot(inner.astype(jnp.float32), linv_diag.T.astype(jnp.float32), preferred_element_type=jnp.float32).astype(jnp.bfloat16)
    half_term = 0.5 * jnp.dot(l_panel.astype(jnp.float32), congruent.astype(jnp.float32), preferred_element_type=jnp.float32)
    solved = jnp.dot(a_panel.astype(jnp.float32), linv_diag.T.astype(jnp.float32), preferred_element_type=jnp.float32)
    first_pass = (solved - half_term).astype(jnp.bfloat16)

    def one_block(pieces):
        a_rows, h_rows, l_rows = pieces
        update = jnp.dot(h_rows.astype(jnp.float32), l_panel.T.astype(jnp.float32), preferred_element_type=jnp.float32)
        update = update + jnp.dot(l_rows.astype(jnp.float32), first_pass.T.astype(jnp.float32), preferred_element_type=jnp.float32)
        return (a_rows.astype(jnp.float32) - update).astype(jnp.bfloat16)
    c_trail = lax.map(one_block, (a_trail.reshape(N_ROW, M // N_ROW, M), first_pass.reshape(N_ROW, M // N_ROW, NB), l_panel.reshape(N_ROW, M // N_ROW, NB))).reshape(M, M)
    finished = (first_pass.astype(jnp.float32) - half_term).astype(jnp.bfloat16)
    panel_bits = finished[:, :BW]
    column_block = panel_bits.astype(jnp.float32)
    gram = jnp.dot(panel_bits.T.astype(jnp.float32), panel_bits.astype(jnp.float32), preferred_element_type=jnp.float32)
    lower = jnp.linalg.cholesky(gram * (1.0 / M))
    q_block = jax.scipy.linalg.solve_triangular(lower, column_block.T, lower=True).T
    return (c_trail, finished, congruent, lower.T, q_block)
```

```python
import functools

import jax
import jax.numpy as jnp
from jax import lax
from jax.experimental import pallas as pl
from jax.experimental.pallas import tpu as pltpu
from jax.sharding import PartitionSpec as P

BW = 256
PANEL = 16
X_COUNT, Z_COUNT = 4, 8
VMEM_LIMIT = 48 * 1024 * 1024

f32, bf16 = jnp.float32, jnp.bfloat16


def dot(left, right, left_dim, right_dim):
    return lax.dot_general(
        left, right, (((left_dim,), (right_dim,)), ((), ())), preferred_element_type=f32
    )


def spread(block, axis, count, groups=None):
    return lax.all_to_all(
        jnp.broadcast_to(block[None], (count,) + block.shape), axis, 0, 0, axis_index_groups=groups
    )


def panel_kernel(diag, rows, first, panel, panel_cols, congruent, gram):
    order = diag.shape[3]
    a_diag = diag[:, 0].reshape(order, order)
    linv = diag[:, 1].reshape(order, order)
    width = rows.shape[3]
    a_rows = rows[:, 0].reshape(order, width)
    l_rows = rows[:, 1].reshape(order, width)
    inner = dot(linv, a_diag, 1, 0).astype(bf16)
    c = dot(inner, linv, 1, 1).astype(bf16)
    congruent[...] = c
    half = 0.5 * dot(c, l_rows, 0, 0)
    f = (dot(linv, a_rows, 1, 0) - half).astype(bf16)
    first[...] = f
    p = (f.astype(f32) - half).astype(bf16)
    panel[...] = p
    own = panel_cols.shape[0]
    start = pl.multiple_of(lax.axis_index("col") * own, own)
    panel_cols[...] = panel[pl.ds(start, own), :]
    band = gram.shape[0]
    gram[...] = dot(p[:band], p[:band], 1, 1)


def split(x):
    high = x.astype(bf16)
    rest = x - high.astype(f32)
    middle = rest.astype(bf16)
    low = (rest - middle.astype(f32)).astype(bf16)
    return high, middle, low


def factor_kernel(scale, gram, panel, r_rows, q_cols, g, w):
    band = g.shape[0]
    g[...] = gram[...].reshape(band, band) * scale
    row_id = lax.broadcasted_iota(jnp.int32, (band, band), 0)
    col_id = lax.broadcasted_iota(jnp.int32, (band, band), 1)
    w[...] = jnp.where(row_id == col_id, 1.0, 0.0)
    sub = lax.broadcasted_iota(jnp.int32, (PANEL, 128), 0)
    for s in range(0, band, PANEL):
        left = s // 128 * 128
        right = (s // 128 + 1) * 128
        rows = pl.ds(s, PANEL)
        parts = [g[rows, pl.ds(o, 128)] for o in range(left, band, 128)]
        n_g = len(parts)
        parts += [w[rows, pl.ds(o, 128)] for o in range(0, right, 128)]
        cols = [
            jnp.broadcast_to(parts[0][:, s - left + t : s - left + t + 1], (PANEL, 128))
            for t in range(PANEL)
        ]
        pivots = jnp.zeros((PANEL, 128), f32)
        for j in range(PANEL):
            pivot = cols[j][j : j + 1, :]
            pivots = jnp.where(sub == j, pivot, pivots)
            if j == PANEL - 1:
                break
            m = jnp.where(sub > j, cols[j] * (1.0 / pivot), 0.0)
            for t in range(j + 1, PANEL):
                cols[t] = cols[t] - m * cols[t][j : j + 1, :]
            parts = [part - m * part[j : j + 1, :] for part in parts]
        root = lax.rsqrt(pivots)
        parts = [part * root for part in parts]
        for i, o in enumerate(range(left, band, 128)):
            g[rows, pl.ds(o, 128)] = parts[i]
        for i, o in enumerate(range(0, right, 128)):
            w[rows, pl.ds(o, 128)] = parts[n_g + i]
        done = s + PANEL
        if done == band:
            break
        top = done // 128 * 128
        u = jnp.concatenate(parts, axis=1)
        h, m, l = split(u)
        a = top - left
        b = band - left
        lefts = jnp.concatenate([x[:, a:b] for x in (h, h, m, h, m, l)], axis=0)
        rights = jnp.concatenate([h, m, h, l, m, h], axis=0)
        update = dot(lefts, rights, 0, 0)[done - top :]
        rest = pl.ds(done, band - done)
        g[rest, pl.ds(left, band - left)] = g[rest, pl.ds(left, band - left)] - update[:, :b]
        w[rest, pl.ds(0, right)] = w[rest, pl.ds(0, right)] - update[:, b:]
    count = q_cols.shape[0]
    start = pl.multiple_of(lax.axis_index("col") * count, count)
    inverse = jnp.concatenate(list(split(w[pl.ds(start, count), :])), axis=0)
    q = dot(inverse, panel[...], 1, 0)
    q_cols[...] = q[:count] + q[count : 2 * count] + q[2 * count :]
    own = r_rows.shape[0]
    start = pl.multiple_of(lax.axis_index("row") * own, own)
    column = lax.broadcasted_iota(jnp.int32, (own, band), 1)
    row = lax.broadcasted_iota(jnp.int32, (own, band), 0) + start
    r_rows[...] = jnp.where(column >= row, g[pl.ds(start, own), :], 0.0)


def trail_kernel(diag, congruent, rows, first, cols, a_trail, c_trail):
    order = diag.shape[3]
    linv = diag[:, 1].reshape(order, order)
    width = cols.shape[3]
    a_cols = cols[:, 0].reshape(order, width)
    l_cols = cols[:, 1].reshape(order, width)
    half = 0.5 * dot(congruent[...], l_cols, 0, 0)
    first_cols = (dot(linv, a_cols, 1, 0) - half).astype(bf16)
    l_rows = rows[:, 1].reshape(order, rows.shape[3])
    update = dot(first[...], l_cols, 0, 0) + dot(l_rows, first_cols, 0, 0)
    c_trail[...] = (a_trail[...].astype(f32) - update).astype(bf16)


def call(kernel, outs, *operands, scratch=()):
    return pl.pallas_call(
        kernel,
        out_shape=[jax.ShapeDtypeStruct(shape, dtype) for shape, dtype in outs],
        in_specs=[pl.BlockSpec(memory_space=pltpu.VMEM)] * len(operands),
        out_specs=[pl.BlockSpec(memory_space=pltpu.VMEM)] * len(outs),
        scratch_shapes=list(scratch),
        compiler_params=pltpu.CompilerParams(vmem_limit_bytes=VMEM_LIMIT),
    )(*operands)


def body(a_trail, a_panel, l_panel, a_diag, linv_diag):
    row_count = lax.axis_size("row")
    col_count = lax.axis_size("col")
    row_index = lax.axis_index("row")
    col_index = lax.axis_index("col")
    x_index, z_index = col_index // Z_COUNT, col_index % Z_COUNT
    z_groups = [[x * Z_COUNT + z for z in range(Z_COUNT)] for x in range(X_COUNT)]
    x_groups = [[x * Z_COUNT + z for x in range(X_COUNT)] for z in range(Z_COUNT)]
    height, own = a_panel.shape
    order = a_diag.shape[1]
    width = a_trail.shape[1]

    diag = lax.all_gather(jnp.stack((a_diag, linv_diag)), "row", axis=0)

    pair = jnp.stack((a_panel.T, l_panel.T))
    by_z = spread(pair, "col", Z_COUNT, z_groups)
    rows = spread(by_z, "col", X_COUNT, x_groups).reshape(col_count, 2, own, height)

    halves = height // width
    piece = Z_COUNT // (Z_COUNT // halves)
    per = Z_COUNT // halves
    half_index, quarter = z_index // per, z_index % per
    share = lax.dynamic_slice(
        by_z, (quarter * piece, 0, 0, half_index * width), (piece, 2, own, width)
    )
    moves = []
    for r in range(row_count):
        for c in range(col_count):
            x, z = c // Z_COUNT, c % Z_COUNT
            target = (x * per + z % per) * col_count + r * halves + z // per
            moves.append((r * col_count + c, target))
    share = lax.ppermute(share, ("row", "col"), moves)
    cols = lax.all_gather(share, "row", axis=0).reshape(col_count, 2, own, width)

    first, panel, panel_cols, congruent, gram = call(
        panel_kernel,
        [
            ((order, height), bf16),
            ((order, height), bf16),
            ((own, height), bf16),
            ((order, order), bf16),
            ((BW, BW), f32),
        ],
        diag,
        rows,
    )
    parts = lax.all_to_all(gram.reshape(row_count, BW // row_count, BW), "row", 0, 0)
    gram = spread(parts.sum(axis=0), "row", row_count)
    r_rows, q_cols = call(
        functools.partial(factor_kernel, 1.0 / (height * row_count)),
        [((BW // row_count, BW), f32), ((BW // col_count, height), f32)],
        gram,
        panel[:BW],
        scratch=[pltpu.VMEM((BW, BW), f32), pltpu.VMEM((BW, BW), f32)],
    )
    (c_trail,) = call(
        trail_kernel,
        [(a_trail.shape, bf16)],
        diag,
        congruent,
        rows,
        first,
        cols,
        a_trail,
    )
    band_cols = BW // col_count
    r_band = lax.dynamic_slice_in_dim(r_rows, col_index * band_cols, band_cols, 1)
    diag_rows = a_diag.shape[0]
    c_diag = lax.dynamic_slice(
        congruent, (row_index * diag_rows, col_index * own), (diag_rows, own)
    )
    return (c_trail, panel_cols.T, c_diag, r_band, q_cols.T)


def solution(mesh):
    both = P("row", "col")
    return jax.shard_map(
        body,
        mesh=mesh,
        in_specs=(both, both, both, P("row", None), P("row", None)),
        out_specs=(both, both, both, both, both),
        check_vma=False,
    )
```

```python
import functools

import jax
import jax.numpy as jnp
from jax import lax
from jax.experimental import pallas as pl
from jax.experimental.pallas import tpu as pltpu
from jax.sharding import PartitionSpec as P

BW = 256
PANEL = 16
STEP = 128
X_COUNT, Z_COUNT = 4, 8
VMEM_LIMIT = 62 * 1024 * 1024

f32, bf16 = jnp.float32, jnp.bfloat16


def dot(left, right, left_dim, right_dim):
    return lax.dot_general(
        left, right, (((left_dim,), (right_dim,)), ((), ())), preferred_element_type=f32
    )


def spread(block, axis, count, groups=None):
    return lax.all_to_all(
        jnp.broadcast_to(block[None], (count,) + block.shape), axis, 0, 0, axis_index_groups=groups
    )


def start(*pairs, sem):
    copies = [pltpu.make_async_copy(*pair, sem.at[i]) for i, pair in enumerate(pairs)]
    for copy in copies:
        copy.start()
    return copies


def wait(copies):
    for copy in copies:
        copy.wait()


def diag_kernel(diag, c_diag, congruent, diag_in, c_out, sem):
    order = diag.shape[3]
    own, wide = c_diag.shape
    wait(start((diag, diag_in), sem=sem))
    a_diag = diag_in[:, 0].reshape(order, order)
    linv = diag_in[:, 1].reshape(order, order)
    inner = dot(linv, a_diag, 1, 0).astype(bf16)
    c_out[...] = dot(inner, linv, 1, 1).astype(bf16)
    copies = start((c_out, congruent), sem=sem)
    col = lax.axis_index("col")
    per = diag.shape[2] // own
    offset = pl.multiple_of(lax.rem(col, per) * own, own)
    linv_rows = diag_in[lax.div(col, per), 1, pl.ds(offset, own), :]
    c_rows = dot(linv_rows, inner, 1, 1).astype(bf16)
    target = lax.broadcasted_iota(jnp.int32, (order, wide), 1) + lax.axis_index("row") * wide
    pick = (lax.broadcasted_iota(jnp.int32, (order, wide), 0) == target).astype(bf16)
    c_diag[...] = dot(c_rows, pick, 1, 0).astype(bf16)
    wait(copies)


def band_kernel(
    diag, congruent, rows, first, panel, gram,
    linv_in, c_in, a_in, l_in, first_out, panel_out, gram_rows, sem,
):
    order, width = congruent.shape[0], rows.shape[3]
    band = panel.shape[0]
    blocks, pieces = band // diag.shape[2], band // rows.shape[2]
    copies = start(
        (rows.at[:, 1], l_in),
        (congruent.at[:, pl.ds(0, band)], c_in),
        (rows.at[pl.ds(0, pieces), 0], a_in),
        (diag.at[pl.ds(0, blocks), 1, :, pl.ds(0, band)], linv_in),
        sem=sem,
    )
    wait(copies[:2])
    half = 0.5 * dot(c_in[...], l_in[...].reshape(order, width), 0, 0)
    wait(copies[2:])
    solved = dot(linv_in[...].reshape(band, band), a_in[...].reshape(band, width), 1, 0)
    f = (solved - half).astype(bf16)
    first_out[...] = f
    p = (f.astype(f32) - half).astype(bf16)
    panel_out[...] = p
    copies = start((first_out, first), (panel_out, panel), sem=sem)
    copy_count, count = gram.shape[:2]
    per = 16 // count
    col = lax.axis_index("col")
    top = panel_out[pl.ds(pl.multiple_of(lax.div(col, per) * 16, 16), 16), :]
    gram_rows[...] = dot(top, p, 1, 1)
    own = gram_rows[pl.ds(pl.multiple_of(lax.rem(col, per) * count, count), count), :]
    for i in range(copy_count):
        gram[i] = own
    wait(copies)


def rest_kernel(
    diag, congruent, rows, panel, first, panel_cols,
    linv_in, c_in, rows_in, first_out, panel_all, sem,
):
    order, width = congruent.shape[0], rows.shape[3]
    band, own = panel.shape[0], panel_cols.shape[0]
    left = order - band
    blocks = band // diag.shape[2]
    copies = start(
        (rows, rows_in),
        (congruent.at[:, pl.ds(band, left)], c_in),
        (diag.at[pl.ds(blocks, diag.shape[0] - blocks), 1], linv_in),
        (panel, panel_all.at[pl.ds(0, band)]),
        sem=sem,
    )
    wait(copies)
    half = 0.5 * dot(c_in[...], rows_in[:, 1].reshape(order, width), 0, 0)
    solved = dot(linv_in[...].reshape(left, order), rows_in[:, 0].reshape(order, width), 1, 0)
    f = (solved - half).astype(bf16)
    first_out[...] = f
    copies = start((first_out, first), sem=sem)
    panel_all[pl.ds(band, left), :] = (f.astype(f32) - half).astype(bf16)
    offset = pl.multiple_of(lax.axis_index("col") * own, own)
    panel_cols[...] = panel_all[pl.ds(offset, own), :]
    wait(copies)


def split(x):
    high = x.astype(bf16)
    rest = x - high.astype(f32)
    middle = rest.astype(bf16)
    low = (rest - middle.astype(f32)).astype(bf16)
    return high, middle, low


def eliminate(scale, gram, g, w, beside):
    band = g.shape[0]
    g[...] = gram[...].reshape(band, band) * scale
    row_id = lax.broadcasted_iota(jnp.int32, (band, band), 0)
    col_id = lax.broadcasted_iota(jnp.int32, (band, band), 1)
    w[...] = jnp.where(row_id == col_id, 1.0, 0.0)
    tall = 2 * PANEL
    sub = lax.broadcasted_iota(jnp.int32, (tall, 128), 0)

    def load(row, size, lefts, rights):
        rows = pl.ds(row, size)
        return [g[rows, pl.ds(o, 128)] for o in lefts] + [w[rows, pl.ds(o, 128)] for o in rights]

    parts = load(0, tall, range(0, band, 128), range(0, 128, 128))
    for s in range(0, band, PANEL):
        left = s // 128 * 128
        right = (s // 128 + 1) * 128
        n_g = (band - left) // 128
        size = parts[0].shape[0]
        cols = [
            jnp.broadcast_to(parts[0][:, s - left + t : s - left + t + 1], (size, 128))
            for t in range(PANEL)
        ]
        pivots = jnp.zeros((PANEL, 128), f32)
        for j in range(PANEL):
            pivot = cols[j][j : j + 1, :]
            pivots = jnp.where(sub[:PANEL] == j, pivot, pivots)
            m = jnp.where(sub[:size] > j, cols[j] * (1.0 / pivot), 0.0)
            for t in range(j + 1, PANEL):
                cols[t] = cols[t] - m * cols[t][j : j + 1, :]
            parts = [part - m * part[j : j + 1, :] for part in parts]
        root = lax.rsqrt(pivots)
        near = [part[PANEL:] for part in parts]
        parts = [part[:PANEL] * root for part in parts]
        beside(s // PANEL)
        rows = pl.ds(s, PANEL)
        for i, o in enumerate(range(left, band, 128)):
            g[rows, pl.ds(o, 128)] = parts[i]
        for i, o in enumerate(range(0, right, 128)):
            w[rows, pl.ds(o, 128)] = parts[n_g + i]
        done = s + PANEL
        if done == band:
            break
        top = done // 128 * 128
        if top > left:
            near = near[1:] + [w[pl.ds(done, PANEL), pl.ds(right, 128)]]
        far = s + tall
        if far == band:
            parts = near
            continue
        u = jnp.concatenate(parts, axis=1)
        h, m, l = split(u)
        base = far // 128 * 128
        a, b = base - left, band - left
        lefts = jnp.concatenate([x[:, a:b] for x in (h, h, m, h, m, l)], axis=0)
        rights = jnp.concatenate([h, m, h, l, m, h], axis=0)
        update = dot(lefts, rights, 0, 0)[far - base :]
        entering = load(far, PANEL, range(top, band, 128), range(0, right, 128))
        entering = [
            x - update[:PANEL, o : o + 128]
            for x, o in zip(entering, range(top - left, update.shape[1], 128))
        ]
        if top > left:
            entering += [w[pl.ds(far, PANEL), pl.ds(right, 128)]]
        parts = [jnp.concatenate(pair, axis=0) for pair in zip(near, entering)]
        far += PANEL
        if far == band:
            continue
        rows = pl.ds(far, band - far)
        for o in range(top, band, 128):
            lanes = pl.ds(o, 128)
            g[rows, lanes] = g[rows, lanes] - update[PANEL:, o - left : o - left + 128]
        for o in range(0, right, 128):
            lanes = pl.ds(o, 128)
            w[rows, lanes] = w[rows, lanes] - update[PANEL:, b + o : b + o + 128]


def finish_kernel(
    scale, gram, panel, diag, congruent, rows, first_top, first_rest, cols, a_trail,
    r_cols, q_cols, c_trail,
    g, w, panel_in, linv_in, c_in, l_in, first_in, cols_in, a_in, first_cols, out, sem, out_sem,
):
    order = diag.shape[3]
    height = rows.shape[3]
    width = cols.shape[3]
    top = first_top.shape[0]
    copies = start(
        (cols, cols_in),
        (diag.at[:, 1], linv_in),
        (congruent, c_in),
        (first_top, first_in.at[pl.ds(0, top)]),
        (first_rest, first_in.at[pl.ds(top, order - top)]),
        (rows.at[:, 1], l_in),
        (a_trail, a_in),
        (panel, panel_in),
        sem=sem,
    )
    outs = []

    def first_of_columns():
        wait(copies[:3])
        a_cols = cols_in[:, 0].reshape(order, width)
        half = 0.5 * dot(c_in[...], cols_in[:, 1].reshape(order, width), 0, 0)
        solved = dot(linv_in[...].reshape(order, order), a_cols, 1, 0)
        first_cols[...] = (solved - half).astype(bf16)

    def trail(i):
        if i == 0:
            wait(copies[3:7])
        part = pl.ds(i * STEP, STEP)
        l_rows = l_in[:, :, part].reshape(order, STEP)
        update = dot(first_in[:, part], cols_in[:, 1].reshape(order, width), 0, 0)
        update += dot(l_rows, first_cols[...], 0, 0)
        out[part] = (a_in[part].astype(f32) - update).astype(bf16)
        outs.extend(start((out.at[part], c_trail.at[part]), sem=out_sem.at[pl.ds(i, 1)]))

    def beside(i):
        if i == 1:
            first_of_columns()
        if 2 <= i < 2 + height // STEP:
            trail(i - 2)

    eliminate(scale, gram, g, w, beside)
    band = g.shape[0]
    count = q_cols.shape[0]
    offset = pl.multiple_of(lax.axis_index("col") * count, count)
    inverse = jnp.concatenate(list(split(w[pl.ds(offset, count), :])), axis=0)
    wait(copies[7:])
    q = dot(inverse, panel_in[...], 1, 0)
    q_cols[...] = q[:count] + q[count : 2 * count] + q[2 * count :]
    own = r_cols.shape[1]
    offset = pl.multiple_of(lax.axis_index("row") * own, own)
    column = lax.broadcasted_iota(jnp.int32, (own, band), 1)
    row = lax.broadcasted_iota(jnp.int32, (own, band), 0) + offset
    upper = jnp.where(column >= row, g[pl.ds(offset, own), :], 0.0)
    target = lax.broadcasted_iota(jnp.int32, (count, band), 0) + lax.axis_index("col") * count
    pick = (lax.broadcasted_iota(jnp.int32, (count, band), 1) == target).astype(bf16)
    high, middle, low = (dot(pick, x, 1, 1) for x in split(upper))
    r_cols[...] = high + (middle + low)
    wait(outs)


def call(kernel, cost, ins, outs, *operands, scratch=()):
    return pl.pallas_call(
        kernel,
        out_shape=[jax.ShapeDtypeStruct(shape, dtype) for _, shape, dtype in outs],
        in_specs=[pl.BlockSpec(memory_space=space) for space in ins],
        out_specs=[pl.BlockSpec(memory_space=space) for space, _, _ in outs],
        scratch_shapes=list(scratch),
        cost_estimate=pl.CostEstimate(flops=cost, bytes_accessed=cost // 500, transcendentals=0),
        compiler_params=pltpu.CompilerParams(vmem_limit_bytes=VMEM_LIMIT),
    )(*operands)


def body(a_trail, a_panel, l_panel, a_diag, linv_diag):
    row_count = lax.axis_size("row")
    col_count = lax.axis_size("col")
    col_index = lax.axis_index("col")
    x_index, z_index = col_index // Z_COUNT, col_index % Z_COUNT
    z_groups = [[x * Z_COUNT + z for z in range(Z_COUNT)] for x in range(X_COUNT)]
    x_groups = [[x * Z_COUNT + z for x in range(X_COUNT)] for z in range(Z_COUNT)]
    height, own = a_panel.shape
    order = a_diag.shape[1]
    width = a_trail.shape[1]

    diag = lax.all_gather(jnp.stack((a_diag, linv_diag)), "row", axis=0)

    pair = jnp.stack((a_panel.T, l_panel.T))
    by_z = spread(pair, "col", Z_COUNT, z_groups)
    rows = spread(by_z, "col", X_COUNT, x_groups).reshape(col_count, 2, own, height)

    halves = height // width
    piece = Z_COUNT // (Z_COUNT // halves)
    per = Z_COUNT // halves
    half_index, quarter = z_index // per, z_index % per
    share = lax.dynamic_slice(
        by_z, (quarter * piece, 0, 0, half_index * width), (piece, 2, own, width)
    )
    moves = []
    for r in range(row_count):
        for c in range(col_count):
            x, z = c // Z_COUNT, c % Z_COUNT
            target = (x * per + z % per) * col_count + r * halves + z // per
            moves.append((r * col_count + c, target))
    share = lax.ppermute(share, ("row", "col"), moves)
    cols = lax.all_gather(share, "row", axis=0).reshape(col_count, 2, own, width)

    HBM, VMEM = pltpu.HBM, pltpu.VMEM
    band_rows, band_cols = BW // row_count, BW // col_count
    diag_rows = a_diag.shape[0]
    sems = pltpu.SemaphoreType.DMA
    c_diag, congruent = call(
        diag_kernel,
        2 * 2 * order**3,
        [HBM],
        [(VMEM, (own, diag_rows), bf16), (HBM, (order, order), bf16)],
        diag,
        scratch=[VMEM(diag.shape, bf16), VMEM((order, order), bf16), sems((1,))],
    )
    first_top, panel_top, gram = call(
        band_kernel,
        2 * 2 * order * height * BW,
        [HBM] * 3,
        [
            (HBM, (BW, height), bf16),
            (HBM, (BW, height), bf16),
            (VMEM, (row_count, band_cols, BW), f32),
        ],
        diag,
        congruent,
        rows,
        scratch=[
            VMEM((BW // diag_rows, diag_rows, BW), bf16),
            VMEM((order, BW), bf16),
            VMEM((BW // own, own, height), bf16),
            VMEM((col_count, own, height), bf16),
            VMEM((BW, height), bf16),
            VMEM((BW, height), bf16),
            VMEM((16, BW), f32),
            sems((4,)),
        ],
    )
    left = order - BW
    first_rest, panel_cols = call(
        rest_kernel,
        2 * 2 * order * height * left,
        [HBM] * 4,
        [(HBM, (left, height), bf16), (VMEM, (own, height), bf16)],
        diag,
        congruent,
        rows,
        panel_top,
        scratch=[
            VMEM((left // diag_rows, diag_rows, order), bf16),
            VMEM((order, left), bf16),
            VMEM(rows.shape, bf16),
            VMEM((left, height), bf16),
            VMEM((order, height), bf16),
            sems((4,)),
        ],
    )
    gram = lax.all_to_all(gram, "row", 0, 0).sum(axis=0)
    gram = spread(gram, "col", col_count)
    r_cols, q_cols, c_trail = call(
        functools.partial(finish_kernel, 1.0 / (height * row_count)),
        2 * 2 * (height + width) * width * order,
        [VMEM] + [HBM] * 8,
        [
            (VMEM, (band_cols, band_rows), f32),
            (VMEM, (band_cols, height), f32),
            (HBM, a_trail.shape, bf16),
        ],
        gram,
        panel_top,
        diag,
        congruent,
        rows,
        first_top,
        first_rest,
        cols,
        a_trail,
        scratch=[
            VMEM((BW, BW), f32),
            VMEM((BW, BW), f32),
            VMEM((BW, height), bf16),
            VMEM((row_count, diag_rows, order), bf16),
            VMEM((order, order), bf16),
            VMEM((col_count, own, height), bf16),
            VMEM((order, height), bf16),
            VMEM(cols.shape, bf16),
            VMEM(a_trail.shape, bf16),
            VMEM((order, width), bf16),
            VMEM(a_trail.shape, bf16),
            sems((8,)),
            sems((height // STEP,)),
        ],
    )
    return (c_trail, panel_cols.T, c_diag.T, r_cols.T, q_cols.T)


def solution(mesh):
    both = P("row", "col")
    return jax.shard_map(
        body,
        mesh=mesh,
        in_specs=(both, both, both, P("row", None), P("row", None)),
        out_specs=(both, both, both, both, both),
        check_vma=False,
    )
```

```python
import functools

import jax
import jax.numpy as jnp
from jax import lax
from jax.experimental import pallas as pl
from jax.experimental.pallas import tpu as pltpu
from jax.sharding import PartitionSpec as P

BW = 256
PANEL = 16
STEP = 128
X_COUNT, Z_COUNT = 4, 8
VMEM_LIMIT = 62 * 1024 * 1024

f32, bf16 = jnp.float32, jnp.bfloat16


def dot(left, right, left_dim, right_dim):
    return lax.dot_general(
        left, right, (((left_dim,), (right_dim,)), ((), ())), preferred_element_type=f32
    )


def spread(block, axis, count, groups=None):
    return lax.all_to_all(
        jnp.broadcast_to(block[None], (count,) + block.shape), axis, 0, 0, axis_index_groups=groups
    )


def start(*pairs, sem):
    copies = [pltpu.make_async_copy(*pair, sem.at[i]) for i, pair in enumerate(pairs)]
    for copy in copies:
        copy.start()
    return copies


def wait(copies):
    for copy in copies:
        copy.wait()


def prepare_kernel(a_diag, linv_diag, a_panel, l_panel, diag, pairs, diag_in, pair_in, sem, out_sem):
    copies = start(
        (a_diag, diag_in.at[0]),
        (linv_diag, diag_in.at[1]),
        (a_panel, pair_in.at[0]),
        (l_panel, pair_in.at[1]),
        sem=sem,
    )
    wait(copies)
    outs = [(diag_in, diag)] + [(pair_in, pairs.at[i]) for i in range(pairs.shape[0])]
    wait(start(*outs, sem=out_sem))


def diag_kernel(diag, c_diag, turned, diag_in, turned_out, sem):
    order = diag.shape[3]
    own, wide = c_diag.shape
    wait(start((diag, diag_in), sem=sem))
    a_diag = diag_in[:, 0].reshape(order, order)
    linv = diag_in[:, 1].reshape(order, order)
    inner = dot(linv, a_diag, 1, 0).astype(bf16)
    turned_out[...] = dot(linv, inner, 1, 1).astype(bf16)
    copies = start((turned_out, turned), sem=sem)
    offset = pl.multiple_of(lax.axis_index("col") * own, own)
    target = lax.broadcasted_iota(jnp.int32, (order, wide), 1) + lax.axis_index("row") * wide
    pick = (lax.broadcasted_iota(jnp.int32, (order, wide), 0) == target).astype(bf16)
    c_diag[...] = dot(turned_out[pl.ds(offset, own), :], pick, 1, 0).astype(bf16)
    wait(copies)


def band_kernel(
    diag, turned, rows, first, panel, gram,
    linv_in, c_in, a_in, l_in, first_out, panel_out, gram_rows, sem,
):
    order, width = turned.shape[0], rows.shape[3]
    band = panel.shape[0]
    blocks, pieces = band // diag.shape[2], band // rows.shape[2]
    copies = start(
        (rows.at[:, 1], l_in),
        (turned.at[pl.ds(0, band)], c_in),
        (rows.at[pl.ds(0, pieces), 0], a_in),
        (diag.at[pl.ds(0, blocks), 1, :, pl.ds(0, band)], linv_in),
        sem=sem,
    )
    wait(copies[:2])
    half = 0.5 * dot(c_in[...], l_in[...].reshape(order, width), 1, 0)
    wait(copies[2:])
    solved = dot(linv_in[...].reshape(band, band), a_in[...].reshape(band, width), 1, 0)
    f = (solved - half).astype(bf16)
    first_out[...] = f
    p = (f.astype(f32) - half).astype(bf16)
    panel_out[...] = p
    copies = start((first_out, first), (panel_out, panel), sem=sem)
    copy_count, count = gram.shape[:2]
    per = 16 // count
    col = lax.axis_index("col")
    top = panel_out[pl.ds(pl.multiple_of(lax.div(col, per) * 16, 16), 16), :]
    gram_rows[...] = dot(top, p, 1, 1)
    own = gram_rows[pl.ds(pl.multiple_of(lax.rem(col, per) * count, count), count), :]
    for i in range(copy_count):
        gram[i] = own
    wait(copies)


def rest_kernel(
    diag, turned, rows, first, panel, first_rows, panel_cols,
    linv_in, c_in, rows_in, first_all, panel_all, first_out, sem,
):
    order, width = turned.shape[0], rows.shape[3]
    band, own = panel.shape[0], panel_cols.shape[0]
    left = order - band
    blocks = band // diag.shape[2]
    copies = start(
        (rows, rows_in),
        (turned.at[pl.ds(band, left)], c_in),
        (diag.at[pl.ds(blocks, diag.shape[0] - blocks), 1], linv_in),
        (first, first_all.at[pl.ds(0, band)]),
        (panel, panel_all.at[pl.ds(0, band)]),
        sem=sem,
    )
    wait(copies)
    half = 0.5 * dot(c_in[...], rows_in[:, 1].reshape(order, width), 1, 0)
    solved = dot(linv_in[...].reshape(left, order), rows_in[:, 0].reshape(order, width), 1, 0)
    f = (solved - half).astype(bf16)
    first_all[pl.ds(band, left), :] = f
    panel_all[pl.ds(band, left), :] = (f.astype(f32) - half).astype(bf16)
    first_out[...] = first_all[...].T
    copies = start((first_out, first_rows), sem=sem)
    offset = pl.multiple_of(lax.axis_index("col") * own, own)
    panel_cols[...] = panel_all[pl.ds(offset, own), :]
    wait(copies)


def turn_kernel(rows, l_rows, l_in, l_out, sem):
    wait(start((rows.at[:, 1], l_in), sem=sem))
    l_out[...] = l_in[...].reshape(l_rows.shape[1], l_rows.shape[0]).T
    wait(start((l_out, l_rows), sem=sem))


def split(x):
    high = x.astype(bf16)
    rest = x - high.astype(f32)
    middle = rest.astype(bf16)
    low = (rest - middle.astype(f32)).astype(bf16)
    return high, middle, low


def eliminate(scale, gram, g, w, beside):
    band = g.shape[0]
    g[...] = gram[...].reshape(band, band) * scale
    row_id = lax.broadcasted_iota(jnp.int32, (band, band), 0)
    col_id = lax.broadcasted_iota(jnp.int32, (band, band), 1)
    w[...] = jnp.where(row_id == col_id, 1.0, 0.0)
    tall = 2 * PANEL
    sub = lax.broadcasted_iota(jnp.int32, (tall, 128), 0)

    def load(row, size, lefts, rights):
        rows = pl.ds(row, size)
        return [g[rows, pl.ds(o, 128)] for o in lefts] + [w[rows, pl.ds(o, 128)] for o in rights]

    parts = load(0, tall, range(0, band, 128), range(0, 128, 128))
    for s in range(0, band, PANEL):
        left = s // 128 * 128
        right = (s // 128 + 1) * 128
        n_g = (band - left) // 128
        size = parts[0].shape[0]
        cols = [
            jnp.broadcast_to(parts[0][:, s - left + t : s - left + t + 1], (size, 128))
            for t in range(PANEL)
        ]
        pivots = jnp.zeros((PANEL, 128), f32)
        for j in range(PANEL):
            pivot = cols[j][j : j + 1, :]
            pivots = jnp.where(sub[:PANEL] == j, pivot, pivots)
            m = jnp.where(sub[:size] > j, cols[j] * (1.0 / pivot), 0.0)
            for t in range(j + 1, PANEL):
                cols[t] = cols[t] - m * cols[t][j : j + 1, :]
            parts = [part - m * part[j : j + 1, :] for part in parts]
        root = lax.rsqrt(pivots)
        near = [part[PANEL:] for part in parts]
        parts = [part[:PANEL] * root for part in parts]
        beside(s // PANEL)
        rows = pl.ds(s, PANEL)
        for i, o in enumerate(range(left, band, 128)):
            g[rows, pl.ds(o, 128)] = parts[i]
        for i, o in enumerate(range(0, right, 128)):
            w[rows, pl.ds(o, 128)] = parts[n_g + i]
        done = s + PANEL
        if done == band:
            break
        top = done // 128 * 128
        if top > left:
            near = near[1:] + [w[pl.ds(done, PANEL), pl.ds(right, 128)]]
        far = s + tall
        if far == band:
            parts = near
            continue
        u = jnp.concatenate(parts, axis=1)
        h, m, l = split(u)
        base = far // 128 * 128
        a, b = base - left, band - left
        lefts = jnp.concatenate([x[:, a:b] for x in (h, h, m, h, m, l)], axis=0)
        rights = jnp.concatenate([h, m, h, l, m, h], axis=0)
        update = dot(lefts, rights, 0, 0)[far - base :]
        entering = load(far, PANEL, range(top, band, 128), range(0, right, 128))
        entering = [
            x - update[:PANEL, o : o + 128]
            for x, o in zip(entering, range(top - left, update.shape[1], 128))
        ]
        if top > left:
            entering += [w[pl.ds(far, PANEL), pl.ds(right, 128)]]
        parts = [jnp.concatenate(pair, axis=0) for pair in zip(near, entering)]
        far += PANEL
        if far == band:
            continue
        rows = pl.ds(far, band - far)
        for o in range(top, band, 128):
            lanes = pl.ds(o, 128)
            g[rows, lanes] = g[rows, lanes] - update[PANEL:, o - left : o - left + 128]
        for o in range(0, right, 128):
            lanes = pl.ds(o, 128)
            w[rows, lanes] = w[rows, lanes] - update[PANEL:, b + o : b + o + 128]


def finish_kernel(
    scale, gram, panel, diag, turned, first, l_rows, cols, a_trail,
    r_cols, q_cols, c_trail,
    g, w, gram_in, panel_in, linv_in, c_in, l_in, first_in, cols_in, a_in, first_cols, out,
    sem, out_sem,
):
    order = diag.shape[3]
    height, width = a_trail.shape
    copies = start(
        (gram, gram_in),
        (cols, cols_in),
        (diag.at[:, 1], linv_in),
        (turned, c_in),
        (first, first_in),
        (l_rows, l_in),
        (a_trail, a_in),
        (panel, panel_in),
        sem=sem,
    )
    outs = []

    def first_of_columns():
        wait(copies[1:4])
        a_cols = cols_in[:, 0].reshape(order, width)
        half = 0.5 * dot(c_in[...], cols_in[:, 1].reshape(order, width), 1, 0)
        solved = dot(linv_in[...].reshape(order, order), a_cols, 1, 0)
        first_cols[...] = (solved - half).astype(bf16)

    def trail(i):
        if i == 0:
            wait(copies[4:7])
        part = pl.ds(i * STEP, STEP)
        update = dot(first_in[part], cols_in[:, 1].reshape(order, width), 1, 0)
        update += dot(l_in[part], first_cols[...], 1, 0)
        out[part] = (a_in[part].astype(f32) - update).astype(bf16)
        outs.extend(start((out.at[part], c_trail.at[part]), sem=out_sem.at[pl.ds(i, 1)]))

    def beside(i):
        if i == 1:
            first_of_columns()
        if 2 <= i < 2 + height // STEP:
            trail(i - 2)

    wait(copies[:1])
    eliminate(scale, gram_in, g, w, beside)
    band = g.shape[0]
    count = q_cols.shape[0]
    offset = pl.multiple_of(lax.axis_index("col") * count, count)
    inverse = jnp.concatenate(list(split(w[pl.ds(offset, count), :])), axis=0)
    wait(copies[7:])
    q = dot(inverse, panel_in[...], 1, 0)
    q_cols[...] = q[:count] + q[count : 2 * count] + q[2 * count :]
    own = r_cols.shape[1]
    offset = pl.multiple_of(lax.axis_index("row") * own, own)
    column = lax.broadcasted_iota(jnp.int32, (own, band), 1)
    row = lax.broadcasted_iota(jnp.int32, (own, band), 0) + offset
    upper = jnp.where(column >= row, g[pl.ds(offset, own), :], 0.0)
    target = lax.broadcasted_iota(jnp.int32, (count, band), 0) + lax.axis_index("col") * count
    pick = (lax.broadcasted_iota(jnp.int32, (count, band), 1) == target).astype(bf16)
    high, middle, low = (dot(pick, x, 1, 1) for x in split(upper))
    r_cols[...] = high + (middle + low)
    wait(outs)


def call(kernel, cost, ins, outs, *operands, scratch=()):
    return pl.pallas_call(
        kernel,
        out_shape=[jax.ShapeDtypeStruct(shape, dtype) for _, shape, dtype in outs],
        in_specs=[pl.BlockSpec(memory_space=space) for space in ins],
        out_specs=[pl.BlockSpec(memory_space=space) for space, _, _ in outs],
        scratch_shapes=list(scratch),
        cost_estimate=pl.CostEstimate(flops=cost, bytes_accessed=cost // 500, transcendentals=0),
        compiler_params=pltpu.CompilerParams(vmem_limit_bytes=VMEM_LIMIT),
    )(*operands)


def body(a_trail, a_panel, l_panel, a_diag, linv_diag):
    row_count = lax.axis_size("row")
    col_count = lax.axis_size("col")
    col_index = lax.axis_index("col")
    x_index, z_index = col_index // Z_COUNT, col_index % Z_COUNT
    z_groups = [[x * Z_COUNT + z for z in range(Z_COUNT)] for x in range(X_COUNT)]
    x_groups = [[x * Z_COUNT + z for x in range(X_COUNT)] for z in range(Z_COUNT)]
    height, own = a_panel.shape
    order = a_diag.shape[1]
    width = a_trail.shape[1]

    HBM, VMEM = pltpu.HBM, pltpu.VMEM
    sems = pltpu.SemaphoreType.DMA
    diag_rows = a_diag.shape[0]
    diag, pairs = call(
        prepare_kernel,
        1 << 20,
        [HBM] * 4,
        [(HBM, (2, diag_rows, order), bf16), (HBM, (Z_COUNT, 2, own, height), bf16)],
        a_diag,
        linv_diag,
        a_panel.T,
        l_panel.T,
        scratch=[
            VMEM((2, diag_rows, order), bf16),
            VMEM((2, own, height), bf16),
            sems((4,)),
            sems((1 + Z_COUNT,)),
        ],
    )
    diag = lax.all_gather(diag, "row", axis=0)
    by_z = lax.all_to_all(pairs, "col", 0, 0, axis_index_groups=z_groups)
    rows = spread(by_z, "col", X_COUNT, x_groups).reshape(col_count, 2, own, height)

    halves = height // width
    piece = Z_COUNT // (Z_COUNT // halves)
    per = Z_COUNT // halves
    half_index, quarter = z_index // per, z_index % per
    share = lax.dynamic_slice(
        by_z, (quarter * piece, 0, 0, half_index * width), (piece, 2, own, width)
    )
    moves = []
    for r in range(row_count):
        for c in range(col_count):
            x, z = c // Z_COUNT, c % Z_COUNT
            target = (x * per + z % per) * col_count + r * halves + z // per
            moves.append((r * col_count + c, target))
    share = lax.ppermute(share, ("row", "col"), moves)
    cols = lax.all_gather(share, "row", axis=0).reshape(col_count, 2, own, width)

    band_rows, band_cols = BW // row_count, BW // col_count
    c_diag, turned = call(
        diag_kernel,
        2 * 2 * order**3,
        [HBM],
        [(VMEM, (own, diag_rows), bf16), (HBM, (order, order), bf16)],
        diag,
        scratch=[VMEM(diag.shape, bf16), VMEM((order, order), bf16), sems((1,))],
    )
    first_top, panel_top, gram = call(
        band_kernel,
        2 * 2 * order * height * BW,
        [HBM] * 3,
        [
            (HBM, (BW, height), bf16),
            (HBM, (BW, height), bf16),
            (VMEM, (row_count, band_cols, BW), f32),
        ],
        diag,
        turned,
        rows,
        scratch=[
            VMEM((BW // diag_rows, diag_rows, BW), bf16),
            VMEM((BW, order), bf16),
            VMEM((BW // own, own, height), bf16),
            VMEM((col_count, own, height), bf16),
            VMEM((BW, height), bf16),
            VMEM((BW, height), bf16),
            VMEM((16, BW), f32),
            sems((4,)),
        ],
    )
    left = order - BW
    first, panel_cols = call(
        rest_kernel,
        2 * 2 * order * height * left,
        [HBM] * 5,
        [(HBM, (height, order), bf16), (VMEM, (own, height), bf16)],
        diag,
        turned,
        rows,
        first_top,
        panel_top,
        scratch=[
            VMEM((left // diag_rows, diag_rows, order), bf16),
            VMEM((left, order), bf16),
            VMEM(rows.shape, bf16),
            VMEM((order, height), bf16),
            VMEM((order, height), bf16),
            VMEM((height, order), bf16),
            sems((5,)),
        ],
    )
    (l_rows,) = call(
        turn_kernel,
        order * height * 1000,
        [HBM],
        [(HBM, (height, order), bf16)],
        rows,
        scratch=[
            VMEM((col_count, own, height), bf16),
            VMEM((height, order), bf16),
            sems((1,)),
        ],
    )
    gram = lax.all_to_all(gram, "row", 0, 0).sum(axis=0)
    gram = spread(gram, "col", col_count)
    r_cols, q_cols, c_trail = call(
        functools.partial(finish_kernel, 1.0 / (height * row_count)),
        2 * 2 * (height + width) * width * order,
        [HBM] * 8,
        [
            (VMEM, (band_cols, band_rows), f32),
            (VMEM, (band_cols, height), f32),
            (HBM, a_trail.shape, bf16),
        ],
        gram,
        panel_top,
        diag,
        turned,
        first,
        l_rows,
        cols,
        a_trail,
        scratch=[
            VMEM((BW, BW), f32),
            VMEM((BW, BW), f32),
            VMEM(gram.shape, f32),
            VMEM((BW, height), bf16),
            VMEM((row_count, diag_rows, order), bf16),
            VMEM((order, order), bf16),
            VMEM((height, order), bf16),
            VMEM((height, order), bf16),
            VMEM(cols.shape, bf16),
            VMEM(a_trail.shape, bf16),
            VMEM((order, width), bf16),
            VMEM(a_trail.shape, bf16),
            sems((8,)),
            sems((height // STEP,)),
        ],
    )
    return (c_trail, panel_cols.T, c_diag.T, r_cols.T, q_cols.T)


def solution(mesh):
    both = P("row", "col")
    return jax.shard_map(
        body,
        mesh=mesh,
        in_specs=(both, both, both, P("row", None), P("row", None)),
        out_specs=(both, both, both, both, both),
        check_vma=False,
    )
```

```python
import functools

import jax
import jax.numpy as jnp
from jax import lax
from jax.experimental import pallas as pl
from jax.experimental.pallas import tpu as pltpu
from jax.sharding import PartitionSpec as P

BW = 256
PANEL = 16
STEP = 128
X_COUNT, Z_COUNT = 4, 8
VMEM_LIMIT = 62 * 1024 * 1024

f32, bf16 = jnp.float32, jnp.bfloat16


def dot(left, right, left_dim, right_dim):
    return lax.dot_general(
        left, right, (((left_dim,), (right_dim,)), ((), ())), preferred_element_type=f32
    )


def spread(block, axis, count, groups=None):
    return lax.all_to_all(
        jnp.broadcast_to(block[None], (count,) + block.shape), axis, 0, 0, axis_index_groups=groups
    )


def start(*pairs, sem):
    copies = [pltpu.make_async_copy(*pair, sem.at[i]) for i, pair in enumerate(pairs)]
    for copy in copies:
        copy.start()
    return copies


def wait(copies):
    for copy in copies:
        copy.wait()


def prepare_kernel(a_diag, linv_diag, a_panel, l_panel, diag, pairs, diag_in, pair_in, sem, out_sem):
    copies = start(
        (a_diag, diag_in.at[0]),
        (linv_diag, diag_in.at[1]),
        (a_panel, pair_in.at[0]),
        (l_panel, pair_in.at[1]),
        sem=sem,
    )
    wait(copies)
    outs = [(diag_in, diag)] + [(pair_in, pairs.at[i]) for i in range(pairs.shape[0])]
    wait(start(*outs, sem=out_sem))


def diag_kernel(diag, c_diag, turned, diag_in, turned_out, sem):
    order = diag.shape[3]
    own, wide = c_diag.shape
    wait(start((diag, diag_in), sem=sem))
    a_diag = diag_in[:, 0].reshape(order, order)
    linv = diag_in[:, 1].reshape(order, order)
    inner = dot(linv, a_diag, 1, 0).astype(bf16)
    turned_out[...] = dot(linv, inner, 1, 1).astype(bf16)
    copies = start((turned_out, turned), sem=sem)
    offset = pl.multiple_of(lax.axis_index("col") * own, own)
    target = lax.broadcasted_iota(jnp.int32, (order, wide), 1) + lax.axis_index("row") * wide
    pick = (lax.broadcasted_iota(jnp.int32, (order, wide), 0) == target).astype(bf16)
    c_diag[...] = dot(turned_out[pl.ds(offset, own), :], pick, 1, 0).astype(bf16)
    wait(copies)


def band_kernel(
    diag, turned, rows, first, panel, gram,
    linv_in, c_in, a_in, l_in, first_out, panel_out, gram_rows, sem,
):
    order, width = turned.shape[0], rows.shape[3]
    band = panel.shape[0]
    blocks, pieces = band // diag.shape[2], band // rows.shape[2]
    copies = start(
        (diag.at[pl.ds(0, blocks), 1, :, pl.ds(0, band)], linv_in),
        (rows.at[pl.ds(0, pieces), 0], a_in),
        (turned.at[pl.ds(0, band)], c_in),
        (rows.at[:, 1], l_in),
        sem=sem,
    )
    wait(copies[:2])
    solved = dot(linv_in[...].reshape(band, band), a_in[...].reshape(band, width), 1, 0)
    wait(copies[2:])
    half = 0.5 * dot(c_in[...], l_in[...].reshape(order, width), 1, 0)
    f = (solved - half).astype(bf16)
    first_out[...] = f
    p = (f.astype(f32) - half).astype(bf16)
    panel_out[...] = p
    copies = start((first_out, first), (panel_out, panel), sem=sem)
    copy_count, count = gram.shape[:2]
    per = 16 // count
    col = lax.axis_index("col")
    top = panel_out[pl.ds(pl.multiple_of(lax.div(col, per) * 16, 16), 16), :]
    gram_rows[...] = dot(top, p, 1, 1)
    own = gram_rows[pl.ds(pl.multiple_of(lax.rem(col, per) * count, count), count), :]
    for i in range(copy_count):
        gram[i] = own
    wait(copies)


def rest_kernel(
    diag, turned, rows, first, panel, first_rows, panel_cols,
    linv_in, c_in, rows_in, first_all, panel_all, first_out, sem,
):
    order, width = turned.shape[0], rows.shape[3]
    band, own = panel.shape[0], panel_cols.shape[0]
    left = order - band
    blocks = band // diag.shape[2]
    copies = start(
        (rows, rows_in),
        (turned.at[pl.ds(band, left)], c_in),
        (diag.at[pl.ds(blocks, diag.shape[0] - blocks), 1], linv_in),
        (first, first_all.at[pl.ds(0, band)]),
        (panel, panel_all.at[pl.ds(0, band)]),
        sem=sem,
    )
    wait(copies)
    half = 0.5 * dot(c_in[...], rows_in[:, 1].reshape(order, width), 1, 0)
    solved = dot(linv_in[...].reshape(left, order), rows_in[:, 0].reshape(order, width), 1, 0)
    f = (solved - half).astype(bf16)
    first_all[pl.ds(band, left), :] = f
    panel_all[pl.ds(band, left), :] = (f.astype(f32) - half).astype(bf16)
    first_out[...] = first_all[...].T
    copies = start((first_out, first_rows), sem=sem)
    offset = pl.multiple_of(lax.axis_index("col") * own, own)
    panel_cols[...] = panel_all[pl.ds(offset, own), :]
    wait(copies)


def turn_kernel(rows, l_rows, l_in, l_out, sem):
    wait(start((rows.at[:, 1], l_in), sem=sem))
    l_out[...] = l_in[...].reshape(l_rows.shape[1], l_rows.shape[0]).T
    wait(start((l_out, l_rows), sem=sem))


def split(x):
    high = x.astype(bf16)
    rest = x - high.astype(f32)
    middle = rest.astype(bf16)
    low = (rest - middle.astype(f32)).astype(bf16)
    return high, middle, low


def eliminate(scale, gram, g, w, beside):
    band = g.shape[0]
    g[...] = gram[...].reshape(band, band) * scale
    row_id = lax.broadcasted_iota(jnp.int32, (band, band), 0)
    col_id = lax.broadcasted_iota(jnp.int32, (band, band), 1)
    w[...] = jnp.where(row_id == col_id, 1.0, 0.0)
    tall = 2 * PANEL
    sub = lax.broadcasted_iota(jnp.int32, (tall, 128), 0)

    def load(row, size, lefts, rights):
        rows = pl.ds(row, size)
        return [g[rows, pl.ds(o, 128)] for o in lefts] + [w[rows, pl.ds(o, 128)] for o in rights]

    parts = load(0, tall, range(0, band, 128), range(0, 128, 128))
    for s in range(0, band, PANEL):
        left = s // 128 * 128
        right = (s // 128 + 1) * 128
        n_g = (band - left) // 128
        size = parts[0].shape[0]
        cols = [
            jnp.broadcast_to(parts[0][:, s - left + t : s - left + t + 1], (size, 128))
            for t in range(PANEL)
        ]
        pivots = jnp.zeros((PANEL, 128), f32)
        for j in range(PANEL):
            pivot = cols[j][j : j + 1, :]
            pivots = jnp.where(sub[:PANEL] == j, pivot, pivots)
            m = jnp.where(sub[:size] > j, cols[j] * (1.0 / pivot), 0.0)
            for t in range(j + 1, PANEL):
                cols[t] = cols[t] - m * cols[t][j : j + 1, :]
            parts = [part - m * part[j : j + 1, :] for part in parts]
        root = lax.rsqrt(pivots)
        near = [part[PANEL:] for part in parts]
        parts = [part[:PANEL] * root for part in parts]
        beside(s // PANEL)
        rows = pl.ds(s, PANEL)
        for i, o in enumerate(range(left, band, 128)):
            g[rows, pl.ds(o, 128)] = parts[i]
        for i, o in enumerate(range(0, right, 128)):
            w[rows, pl.ds(o, 128)] = parts[n_g + i]
        done = s + PANEL
        if done == band:
            break
        top = done // 128 * 128
        if top > left:
            near = near[1:] + [w[pl.ds(done, PANEL), pl.ds(right, 128)]]
        far = s + tall
        if far == band:
            parts = near
            continue
        u = jnp.concatenate(parts, axis=1)
        h, m, l = split(u)
        base = far // 128 * 128
        a, b = base - left, band - left
        lefts = jnp.concatenate([x[:, a:b] for x in (h, h, m, h, m, l)], axis=0)
        rights = jnp.concatenate([h, m, h, l, m, h], axis=0)
        update = dot(lefts, rights, 0, 0)[far - base :]
        entering = load(far, PANEL, range(top, band, 128), range(0, right, 128))
        entering = [
            x - update[:PANEL, o : o + 128]
            for x, o in zip(entering, range(top - left, update.shape[1], 128))
        ]
        if top > left:
            entering += [w[pl.ds(far, PANEL), pl.ds(right, 128)]]
        parts = [jnp.concatenate(pair, axis=0) for pair in zip(near, entering)]
        far += PANEL
        if far == band:
            continue
        rows = pl.ds(far, band - far)
        for o in range(top, band, 128):
            lanes = pl.ds(o, 128)
            g[rows, lanes] = g[rows, lanes] - update[PANEL:, o - left : o - left + 128]
        for o in range(0, right, 128):
            lanes = pl.ds(o, 128)
            w[rows, lanes] = w[rows, lanes] - update[PANEL:, b + o : b + o + 128]


def finish_kernel(
    scale, gram, panel, diag, turned, first, l_rows, cols, a_trail,
    r_cols, q_cols, c_trail,
    g, w, gram_in, panel_in, linv_in, c_in, l_in, first_in, cols_in, a_in, first_cols, out,
    sem, out_sem,
):
    order = diag.shape[3]
    height, width = a_trail.shape
    copies = start(
        (gram, gram_in),
        (cols, cols_in),
        (diag.at[:, 1], linv_in),
        (turned, c_in),
        (first, first_in),
        (l_rows, l_in),
        (a_trail, a_in),
        (panel, panel_in),
        sem=sem,
    )
    outs = []

    def first_of_columns():
        wait(copies[1:4])
        a_cols = cols_in[:, 0].reshape(order, width)
        half = 0.5 * dot(c_in[...], cols_in[:, 1].reshape(order, width), 1, 0)
        solved = dot(linv_in[...].reshape(order, order), a_cols, 1, 0)
        first_cols[...] = (solved - half).astype(bf16)

    def trail(i):
        if i == 0:
            wait(copies[4:7])
        part = pl.ds(i * STEP, STEP)
        update = dot(first_in[part], cols_in[:, 1].reshape(order, width), 1, 0)
        update += dot(l_in[part], first_cols[...], 1, 0)
        out[part] = (a_in[part].astype(f32) - update).astype(bf16)
        outs.extend(start((out.at[part], c_trail.at[part]), sem=out_sem.at[pl.ds(i, 1)]))

    def beside(i):
        if i == 1:
            first_of_columns()
        if 2 <= i < 2 + height // STEP:
            trail(i - 2)

    wait(copies[:1])
    eliminate(scale, gram_in, g, w, beside)
    band = g.shape[0]
    count = q_cols.shape[0]
    offset = pl.multiple_of(lax.axis_index("col") * count, count)
    inverse = jnp.concatenate(list(split(w[pl.ds(offset, count), :])), axis=0)
    wait(copies[7:])
    q = dot(inverse, panel_in[...], 1, 0)
    q_cols[...] = q[:count] + q[count : 2 * count] + q[2 * count :]
    own = r_cols.shape[1]
    offset = pl.multiple_of(lax.axis_index("row") * own, own)
    column = lax.broadcasted_iota(jnp.int32, (own, band), 1)
    row = lax.broadcasted_iota(jnp.int32, (own, band), 0) + offset
    upper = jnp.where(column >= row, g[pl.ds(offset, own), :], 0.0)
    target = lax.broadcasted_iota(jnp.int32, (count, band), 0) + lax.axis_index("col") * count
    pick = (lax.broadcasted_iota(jnp.int32, (count, band), 1) == target).astype(bf16)
    high, middle, low = (dot(pick, x, 1, 1) for x in split(upper))
    r_cols[...] = high + (middle + low)
    wait(outs)


def call(kernel, cost, ins, outs, *operands, scratch=()):
    return pl.pallas_call(
        kernel,
        out_shape=[jax.ShapeDtypeStruct(shape, dtype) for _, shape, dtype in outs],
        in_specs=[pl.BlockSpec(memory_space=space) for space in ins],
        out_specs=[pl.BlockSpec(memory_space=space) for space, _, _ in outs],
        scratch_shapes=list(scratch),
        cost_estimate=pl.CostEstimate(flops=cost, bytes_accessed=cost // 500, transcendentals=0),
        compiler_params=pltpu.CompilerParams(vmem_limit_bytes=VMEM_LIMIT),
    )(*operands)


def body(a_trail, a_panel, l_panel, a_diag, linv_diag):
    row_count = lax.axis_size("row")
    col_count = lax.axis_size("col")
    col_index = lax.axis_index("col")
    x_index, z_index = col_index // Z_COUNT, col_index % Z_COUNT
    z_groups = [[x * Z_COUNT + z for z in range(Z_COUNT)] for x in range(X_COUNT)]
    x_groups = [[x * Z_COUNT + z for x in range(X_COUNT)] for z in range(Z_COUNT)]
    height, own = a_panel.shape
    order = a_diag.shape[1]
    width = a_trail.shape[1]

    HBM, VMEM = pltpu.HBM, pltpu.VMEM
    sems = pltpu.SemaphoreType.DMA
    diag_rows = a_diag.shape[0]
    diag, pairs = call(
        prepare_kernel,
        1 << 20,
        [HBM] * 4,
        [(HBM, (2, diag_rows, order), bf16), (HBM, (Z_COUNT, 2, own, height), bf16)],
        a_diag,
        linv_diag,
        a_panel.T,
        l_panel.T,
        scratch=[
            VMEM((2, diag_rows, order), bf16),
            VMEM((2, own, height), bf16),
            sems((4,)),
            sems((1 + Z_COUNT,)),
        ],
    )
    diag = lax.all_gather(diag, "row", axis=0)
    by_z = lax.all_to_all(pairs, "col", 0, 0, axis_index_groups=z_groups)
    rows = spread(by_z, "col", X_COUNT, x_groups).reshape(col_count, 2, own, height)

    halves = height // width
    piece = Z_COUNT // (Z_COUNT // halves)
    per = Z_COUNT // halves
    half_index, quarter = z_index // per, z_index % per
    share = lax.dynamic_slice(
        by_z, (quarter * piece, 0, 0, half_index * width), (piece, 2, own, width)
    )
    moves = []
    for r in range(row_count):
        for c in range(col_count):
            x, z = c // Z_COUNT, c % Z_COUNT
            target = (x * per + z % per) * col_count + r * halves + z // per
            moves.append((r * col_count + c, target))
    share = lax.ppermute(share, ("row", "col"), moves)
    cols = lax.all_gather(share, "row", axis=0).reshape(col_count, 2, own, width)

    band_rows, band_cols = BW // row_count, BW // col_count
    c_diag, turned = call(
        diag_kernel,
        2 * 2 * order**3,
        [HBM],
        [(VMEM, (own, diag_rows), bf16), (HBM, (order, order), bf16)],
        diag,
        scratch=[VMEM(diag.shape, bf16), VMEM((order, order), bf16), sems((1,))],
    )
    first_top, panel_top, gram = call(
        band_kernel,
        2 * 2 * order * height * BW,
        [HBM] * 3,
        [
            (HBM, (BW, height), bf16),
            (HBM, (BW, height), bf16),
            (VMEM, (row_count, band_cols, BW), f32),
        ],
        diag,
        turned,
        rows,
        scratch=[
            VMEM((BW // diag_rows, diag_rows, BW), bf16),
            VMEM((BW, order), bf16),
            VMEM((BW // own, own, height), bf16),
            VMEM((col_count, own, height), bf16),
            VMEM((BW, height), bf16),
            VMEM((BW, height), bf16),
            VMEM((16, BW), f32),
            sems((4,)),
        ],
    )
    left = order - BW
    first, panel_cols = call(
        rest_kernel,
        2 * 2 * order * height * left,
        [HBM] * 5,
        [(HBM, (height, order), bf16), (VMEM, (own, height), bf16)],
        diag,
        turned,
        rows,
        first_top,
        panel_top,
        scratch=[
            VMEM((left // diag_rows, diag_rows, order), bf16),
            VMEM((left, order), bf16),
            VMEM(rows.shape, bf16),
            VMEM((order, height), bf16),
            VMEM((order, height), bf16),
            VMEM((height, order), bf16),
            sems((5,)),
        ],
    )
    (l_rows,) = call(
        turn_kernel,
        order * height * 1000,
        [HBM],
        [(HBM, (height, order), bf16)],
        rows,
        scratch=[
            VMEM((col_count, own, height), bf16),
            VMEM((height, order), bf16),
            sems((1,)),
        ],
    )
    gram = lax.all_to_all(gram, "row", 0, 0).sum(axis=0)
    gram = spread(gram, "col", col_count)
    r_cols, q_cols, c_trail = call(
        functools.partial(finish_kernel, 1.0 / (height * row_count)),
        2 * 2 * (height + width) * width * order,
        [HBM] * 8,
        [
            (VMEM, (band_cols, band_rows), f32),
            (VMEM, (band_cols, height), f32),
            (HBM, a_trail.shape, bf16),
        ],
        gram,
        panel_top,
        diag,
        turned,
        first,
        l_rows,
        cols,
        a_trail,
        scratch=[
            VMEM((BW, BW), f32),
            VMEM((BW, BW), f32),
            VMEM(gram.shape, f32),
            VMEM((BW, height), bf16),
            VMEM((row_count, diag_rows, order), bf16),
            VMEM((order, order), bf16),
            VMEM((height, order), bf16),
            VMEM((height, order), bf16),
            VMEM(cols.shape, bf16),
            VMEM(a_trail.shape, bf16),
            VMEM((order, width), bf16),
            VMEM(a_trail.shape, bf16),
            sems((8,)),
            sems((height // STEP,)),
        ],
    )
    return (c_trail, panel_cols.T, c_diag.T, r_cols.T, q_cols.T)


def solution(mesh):
    both = P("row", "col")
    return jax.shard_map(
        body,
        mesh=mesh,
        in_specs=(both, both, both, P("row", None), P("row", None)),
        out_specs=(both, both, both, both, both),
        check_vma=False,
    )
```
